32 devices in a mesh: groups: 2 (over x), lon: 16 (over z, y, core).
Axes of the slice: x: 2, y: 2, z: 4, core: 2. Of those that a mesh axis runs over, the one named last changes fastest.
Arguments:
- tokens: bfloat16 [64, 96, 512], P('groups', 'lon'), parts along dimension 0, may hold values from -36 to 36
- input_weight: bfloat16 [512, 1536], replicated, may hold values from -0.25 to 0.25
- output_weight: bfloat16 [512, 512], replicated, may hold values from -0.25 to 0.25
- upstream: bfloat16 [64, 96, 512], P('groups', 'lon'), parts along dimension 0, may hold values from -6 to 6
Outputs:
- token_grads: bfloat16 [64, 96, 512], P('groups', 'lon'), parts along dimension 0
- input_grads: float32 [512, 3072], P('lon', 'groups'), parts along dimension 1
- output_grads: float32 [1024, 512], P('groups', 'lon'), parts along dimension 0
The draws below stay inside these ranges and needn't reach their ends.
There are 2 independent parts, one for each index of `groups`. The reference program is written for one: setup_inputs(seed, part) draws one part's arguments, and reference() takes and returns one part's arrays. A program takes and returns all parts, laid end to end along the dimension named above; an argument that names none is the same for every part. Nothing has to cross between parts.
All inputs are finite; a program needn't handle non-finite values.
Results may differ from the reference program's by a relative error of at most 0.005.
The reference program's roundings to bfloat16 on the way count: a program that leaves them out, or rounds other values in their place, can miss the bound.
Values may be sent and summed in bfloat16 or wider, within the bound.
A program may use at most 64 MiB of HBM per device.

```python
import math
import jax
import jax.numpy as jnp
from jax import lax

D = 512
HEADS = 8
RADIUS = 10
LAT = 32
LON_DEV = 6
HEAD_DIM = 64
NLON = 96
N_LON = 16


def draw_tokens(key, part):
    noise_key, pair_key, scale_key = jax.random.split(jax.random.fold_in(key, 11), 3)
    noise_base = jnp.clip(jax.random.normal(noise_key, (LAT, NLON, D), jnp.float32), -4.0, 4.0)
    pair_order = jax.random.permutation(pair_key, N_LON)
    owner_block = pair_order[jnp.arange(NLON) // LON_DEV]
    column_block = jnp.arange(D) // (D // N_LON)
    boosted = 1.0 + 2.0 * (owner_block[:, None] == column_block[None, :]).astype(jnp.float32)
    row_scale = jnp.exp(jax.random.uniform(scale_key, (LAT, NLON, 1), jnp.float32, math.log(0.5), math.log(2.0)))
    return (noise_base * boosted[None, :, :] * row_scale).astype(jnp.bfloat16)


def raised(entries, stream_key, source, target, blocks, factor):
    owner, partner = [(jnp.arange(entries.shape[axis_at]) // (entries.shape[axis_at] // blocks)).reshape([-1 if axis == axis_at else 1 for axis in range(entries.ndim)]) for axis_at in (source, target)]
    chosen = jax.random.permutation(stream_key, blocks)[partner]
    strong = (owner == chosen) | (owner == (partner + blocks // 2) % blocks)
    return jnp.where(strong, factor * entries, entries)


def block_scale(stream_key, dims, cuts, low, top_value):
    def one(dim, parts):
        draws = jax.random.uniform(jax.random.fold_in(jax.random.fold_in(stream_key, 6), dim), (parts,), jnp.float32, low / len(cuts), top_value / len(cuts))
        return jnp.repeat(jnp.exp(draws), dims[dim] // parts).reshape((-1,) + (1,) * (len(dims) - dim - 1))

    gain = one(*cuts[0])
    for cut in cuts[1:]:
        gain = gain * one(*cut)
    return gain


def normal_values(own_key, extent, scale, reach, cuts=(), kind=jnp.bfloat16):
    values = scale * jax.random.normal(own_key, extent, jnp.float32)
    if cuts:
        values = values * block_scale(own_key, extent, cuts, -0.22, 0.18)
    return jnp.clip(values, -reach, reach).astype(kind)


def bell_draw_with(key, shape, width, most, cuts, heavy, kind=jnp.bfloat16):
    result = width * jax.random.normal(key, shape, jnp.float32)
    if cuts:
        result = result * block_scale(key, shape, cuts, -0.22, 0.18)
    return jnp.clip(raised(result, jax.random.fold_in(key, 3), *heavy), -most, most).astype(kind)


def setup_inputs(seed: int = 0, part: int = 0) -> dict:
    splits = jax.random.split(jax.random.key(seed), 5)
    part_keys = jax.random.split(jax.random.fold_in(splits[4], part), 5)
    return {
        "tokens": draw_tokens(jax.random.fold_in(jax.random.fold_in(splits[4], part), 71), part),
        "input_weight": normal_values(splits[1], (D, 3 * D), D ** -0.5, 0.25),
        "output_weight": normal_values(splits[2], (D, D), D ** -0.5, 0.25),
        "upstream": bell_draw_with(part_keys[3], (LAT, NLON, D), 1.0, 6.0, ((1, 16),), (1, 2, 16, 2.0)),
    }


def window_mask(lat_rows, cols, wide):
    query_lat = jnp.repeat(jnp.arange(lat_rows), cols)
    query_col = jnp.tile(jnp.arange(cols), lat_rows)
    key_lat = jnp.repeat(jnp.arange(lat_rows), wide)
    key_col = jnp.tile(jnp.arange(wide), lat_rows)
    near_lat = jnp.abs(query_lat[:, None] - key_lat[None, :]) <= RADIUS
    near_col = jnp.abs(query_col[:, None] + RADIUS - key_col[None, :]) <= RADIUS
    return near_lat & near_col


def reference(tokens, input_weight, output_weight, upstream):
    f32 = jnp.float32
    low = jnp.bfloat16
    wide = LON_DEV + 2 * RADIUS
    scale = HEAD_DIM ** -0.5
    flat = tokens.reshape(-1, D)
    projected = jnp.dot(flat, input_weight, preferred_element_type=f32).astype(low).reshape(LAT, NLON, 3 * D)
    query = projected[:, :, :D]
    keys = projected[:, :, D:2 * D]
    values = projected[:, :, 2 * D:]
    grad_flat = upstream.reshape(-1, D)
    grad_attn = jnp.dot(grad_flat, output_weight.T, preferred_element_type=f32).astype(low).reshape(LAT, NLON, D)
    mask = window_mask(LAT, LON_DEV, wide)

    def heads_of(array):
        return array.reshape(array.shape[0], HEADS, HEAD_DIM)

    def own(array, block):
        start = (block * LON_DEV).astype(jnp.int32)
        return lax.dynamic_slice_in_dim(array, start, LON_DEV, axis=1).reshape(LAT * LON_DEV, array.shape[2])

    def beside_all(array, block):
        index = ((block * LON_DEV - RADIUS + jnp.arange(wide, dtype=jnp.int32)) % NLON).astype(jnp.int32)
        return jnp.take(array, index, axis=1).reshape(LAT * wide, array.shape[2])

    def first_pass(block):
        q_block = heads_of(own(query, block)).astype(f32)
        k_block = heads_of(beside_all(keys, block)).astype(f32)
        v_block = heads_of(beside_all(values, block)).astype(f32)
        g_block = heads_of(own(grad_attn, block)).astype(f32)
        score = scale * jnp.einsum('qhd,khd->hqk', q_block, k_block)
        score = jnp.where(mask[None], score, -jnp.inf)
        peak = jnp.max(score, axis=2, keepdims=True)
        lse = peak[:, :, 0] + jnp.log(jnp.sum(jnp.exp(score - peak), axis=2))
        probs = jnp.exp(score - lse[:, :, None])
        probs_low = probs.astype(low)
        attended = jnp.einsum('hqk,khd->qhd', probs_low.astype(f32), v_block).astype(low)
        delta = jnp.sum(g_block * attended.astype(f32), axis=2)
        grad_probs = jnp.einsum('qhd,khd->hqk', g_block, v_block)
        grad_score = (probs * (grad_probs - delta.T[:, :, None])).astype(low)
        grad_query = scale * jnp.einsum('hqk,khd->qhd', grad_score.astype(f32), k_block)
        return attended.reshape(-1, D), lse.T, delta, grad_query.reshape(-1, D)

    blocks = jnp.arange(N_LON, dtype=jnp.int32)

    def unblock(array):
        rest = array.shape[2:]
        shaped = array.reshape((N_LON, LAT, LON_DEV) + rest)
        return jnp.moveaxis(shaped, 0, 1).reshape((LAT, NLON) + rest)

    attended, lse, delta, grad_query = lax.map(first_pass, blocks)
    attended = unblock(attended)
    lse = unblock(lse)
    delta = unblock(delta)
    grad_query = unblock(grad_query)

    def second_pass(block):
        q_ext = heads_of(beside_all(query, block)).astype(f32)
        g_ext = heads_of(beside_all(grad_attn, block)).astype(f32)
        lse_ext = beside_all(lse, block)
        delta_ext = beside_all(delta, block)
        k_block = heads_of(own(keys, block)).astype(f32)
        v_block = heads_of(own(values, block)).astype(f32)
        score = scale * jnp.einsum('qhd,khd->hqk', q_ext, k_block)
        score = jnp.where(mask.T[None], score, -jnp.inf)
        probs = jnp.exp(score - lse_ext.T[:, :, None])
        probs_low = probs.astype(low)
        grad_probs = jnp.einsum('qhd,khd->hqk', g_ext, v_block)
        grad_score = (probs * (grad_probs - delta_ext.T[:, :, None])).astype(low)
        grad_key = scale * jnp.einsum('hqk,qhd->khd', grad_score.astype(f32), q_ext)
        grad_value = jnp.einsum('hqk,qhd->khd', probs_low.astype(f32), g_ext)
        return grad_key.reshape(-1, D), grad_value.reshape(-1, D)

    grad_key, grad_value = lax.map(second_pass, blocks)
    grad_key = unblock(grad_key)
    grad_value = unblock(grad_value)
    combined = jnp.concatenate([grad_query, grad_key, grad_value], axis=2).astype(low).reshape(-1, 3 * D)
    token_grads = jnp.dot(combined, input_weight.T, preferred_element_type=f32).astype(low).reshape(LAT, NLON, D)
    input_grads = jnp.dot(flat.T, combined, preferred_element_type=f32)
    output_grads = jnp.dot(attended.reshape(-1, D).T, grad_flat, preferred_element_type=f32)
    return token_grads, input_grads, output_grads
```

```python
import functools

import jax
import jax.numpy as jnp
from jax import lax
from jax.experimental import pallas as pl
from jax.experimental.pallas import tpu as pltpu
from jax.sharding import PartitionSpec as P

HEADS = 8
RADIUS = 10
F32 = jnp.float32
LOW = jnp.bfloat16


def rim_widths(cols):
    hop_count = (RADIUS + cols - 1) // cols
    return [min(cols, RADIUS - (distance - 1) * cols) for distance in range(1, hop_count + 1)]


def segments(cols):
    parts = []
    for distance, count in enumerate(rim_widths(cols), 1):
        parts.append((-distance, count, -(distance - 1) * cols - count, cols - count))
        parts.append((distance, count, distance * cols, 0))
    return parts


def nn(left, right):
    return lax.dot_general(left, right, (((1,), (0,)), ((), ())), preferred_element_type=F32)


def nt(left, right):
    return lax.dot_general(left, right, (((1,), (1,)), ((), ())), preferred_element_type=F32)


def tn(left, right):
    return lax.dot_general(left, right, (((0,), (0,)), ((), ())), preferred_element_type=F32)


def kernel(
    n, lat, cols, staged, x_ref, u_ref, wi_ref, wo_ref, *refs
):
    if staged:
        tg_ref, ig_ref, og_ref = refs[:3]
        refs = refs[3:]
    else:
        tg_ref, term_ref = refs[:2]
        refs = refs[2:]
    xe, xet, ut, kv, qs, gs, dq, dkv, bias, tgs, tgr = refs[:11]
    hs, hr, bs, br = refs[11:15]
    own = lat * cols
    width = x_ref.shape[1]
    parts = segments(cols)
    me = lax.axis_index("lon")
    pairs = width // 128
    half = 64
    scale = half ** (-0.5)

    def at(offset):
        return lax.rem(me + offset + n, n)

    offsets = [part[0] for part in parts]
    if staged:
        tb, ra, sa, rb, sb, rc, sas, sar, sbs, sbr, scs, scr = refs[15:]
        deep = n // 4
        core = lax.rem(me, 2)
        mid = lax.rem(me // 2, 2)
        top = me // 4
        offsets = offsets + [4 * k for k in range(1, deep)]
    barrier = pltpu.get_barrier_semaphore()
    for offset in offsets:
        pl.semaphore_signal(
            barrier, inc=1, device_id={"lon": at(offset)}, device_id_type=pl.DeviceIdType.MESH
        )
    pl.semaphore_wait(barrier, len(offsets))

    def remote(src, dst, send, recv, target):
        return pltpu.make_async_remote_copy(
            src_ref=src,
            dst_ref=dst,
            send_sem=send,
            recv_sem=recv,
            device_id={"lon": target},
            device_id_type=pl.DeviceIdType.MESH,
        )

    halo = []
    start = own
    starts = []
    for index, (hop, count, _, first) in enumerate(parts):
        halo.append(
            remote(
                x_ref.at[pl.ds(first * lat, count * lat)],
                xe.at[pl.ds(start, count * lat)],
                hs.at[index],
                hr.at[index],
                at(-hop),
            )
        )
        starts.append(start)
        start += count * lat
    total = start
    for copy in halo:
        copy.start()

    x_own = x_ref[...]
    xe[0:own, :] = x_own
    qs[...] = (nn(x_own, wi_ref[:, 0:width]).astype(LOW).astype(F32) * scale).astype(LOW)
    gs[...] = nt(u_ref[...], wo_ref[...]).astype(LOW)
    ut[...] = u_ref[...].T
    kv[0:own, :] = nn(x_own, wi_ref[:, width:]).astype(LOW)

    rows2 = lax.broadcasted_iota(jnp.int32, (2 * own, total), 0)
    keys2 = lax.broadcasted_iota(jnp.int32, (2 * own, total), 1)
    rows2 = jnp.where(rows2 >= own, rows2 - own, rows2)
    tile = lax.div(keys2, lat)
    place = tile
    count_before = cols
    for hop, count, first, _ in parts:
        place = jnp.where(tile >= count_before, tile + (first - count_before), place)
        count_before += count
    near_col = jnp.abs(lax.div(rows2, lat) - place) <= RADIUS
    near_lat = jnp.abs(lax.rem(rows2, lat) - lax.rem(keys2, lat)) <= RADIUS
    bias[...] = jnp.where(near_col & near_lat, 0.0, -1e30).astype(F32)

    for copy in halo:
        copy.wait()
    kv[own:total, :] = nn(xe[own:total, :], wi_ref[:, width:]).astype(LOW)
    xet[...] = xe[...].T

    if staged:

        def copy_a(p):
            return remote(
                tb.at[p, 1 - core], ra.at[p], sas.at[p], sar.at[p], me + 1 - 2 * core
            )

        def copy_b(p):
            return remote(
                sa.at[p, 1 - mid], rb.at[p], sbs.at[p], sbr.at[p], me + 2 - 4 * mid
            )

        def copies_c(p):
            out = []
            for k in range(1, deep):
                target = lax.rem(top + k, deep)
                out.append(
                    remote(
                        sb.at[p, target],
                        rc.at[p, k - 1],
                        scs.at[p, k - 1],
                        scr.at[p, k - 1],
                        target * 4 + lax.rem(me, 4),
                    )
                )
            return out

        def stage_b(p):
            copy_a(p).wait()
            mine = tb[p, core].astype(F32) + ra[p].astype(F32)
            sa[p] = mine.astype(LOW).reshape(sa.shape[1:])
            copy_b(p).start()

        def stage_c(p):
            copy_b(p).wait()
            sb[p] = (sa[p, mid].astype(F32) + rb[p].astype(F32)).astype(LOW)
            for copy in copies_c(p):
                copy.start()

        def finish(p):
            for copy in copies_c(p):
                copy.wait()
            done = sa[p, mid, top].astype(F32) + rb[p, top].astype(F32)
            for k in range(1, deep):
                done = done + rc[p, k - 1].astype(F32)
            for k in range(3):
                ig_ref[:, width * k + 128 * p : width * k + 128 * p + 128] = done[
                    :, 128 * k : 128 * k + 128
                ]
            og_ref[:, 128 * p : 128 * p + 128] = done[:, 384:512]

    lane = lax.broadcasted_iota(jnp.int32, (own, 128), 1)

    def stacked(block):
        zero = jnp.zeros_like(block)
        return jnp.concatenate(
            [jnp.where(lane < half, block, zero), jnp.where(lane < half, zero, block)], axis=0
        )

    def picked(block):
        return jnp.where(lane < half, block[0:own], block[own : 2 * own])

    def pair(p, carry):
        here = pl.ds(pl.multiple_of(p * 128, 128), 128)
        there = pl.ds(pl.multiple_of(width + p * 128, 128), 128)
        q2 = stacked(qs[:, here])
        g2 = stacked(gs[:, here])
        k2 = kv[:, here]
        v2 = kv[:, there]
        score = nt(q2, k2) + bias[...]
        peak = jnp.max(score, axis=1, keepdims=True)
        grown = jnp.exp(score - peak)
        probs = grown * (1.0 / jnp.sum(grown, axis=1, keepdims=True))
        low = probs.astype(LOW)
        reached = nn(low, v2).astype(LOW)
        delta = jnp.sum(g2.astype(F32) * reached.astype(F32), axis=1, keepdims=True)
        slope = (probs * (nt(g2, v2) - delta)).astype(LOW)
        dq_p = (picked(nn(slope, k2)) * scale).astype(LOW)
        att_p = picked(reached)
        dk_p = tn(q2, slope).T.astype(LOW)
        dv_p = tn(g2, low).T.astype(LOW)
        dq[:, here] = dq_p
        dkv[:, here] = dk_p
        dkv[:, there] = dv_p
        term_q = nn(xet[:, 0:own], dq_p)
        term_k = nn(xet[...], dk_p)
        term_v = nn(xet[...], dv_p)
        term_o = nn(ut[...], att_p)
        terms = (term_q, term_k, term_v, term_o)
        if staged:
            rows = width // n
            for k, term in enumerate(terms):
                block = term.astype(LOW)
                for j in range(n):
                    tb[p, j % 2, ((j // 2) % 2) * deep + j // 4, :, 128 * k : 128 * k + 128] = (
                        block[rows * j : rows * j + rows]
                    )
            copy_a(p).start()

            @pl.when(p >= 1)
            def _():
                stage_b(p - 1)

            @pl.when(p >= 2)
            def _():
                stage_c(p - 2)
        else:
            for k, term in enumerate(terms):
                term_ref[:, pl.ds(pl.multiple_of(width * k + p * 128, 128), 128)] = term
        return carry

    lax.fori_loop(0, pairs, pair, 0)

    tgs[...] = nt(dkv[own:total, :], wi_ref[:, width:]).astype(LOW)
    back = []
    start = 0
    for index, (hop, count, _, first) in enumerate(parts):
        back.append(
            remote(
                tgs.at[pl.ds(start, count * lat)],
                tgr.at[pl.ds(start, count * lat)],
                bs.at[index],
                br.at[index],
                at(hop),
            )
        )
        start += count * lat
    for copy in back:
        copy.start()
    if staged:
        stage_b(pairs - 1)
        stage_c(pairs - 2)
    mine = nt(dkv[0:own, :], wi_ref[:, width:]) + nt(dq[...], wi_ref[:, 0:width])
    bias[0:own, 0:width] = mine
    if staged:
        stage_c(pairs - 1)
    for copy in back:
        copy.wait()
    start = 0
    for index, (hop, count, _, first) in enumerate(parts):
        spot = slice(first * lat, (first + count) * lat)
        bias[spot, 0:width] += tgr[start : start + count * lat, :].astype(F32)
        start += count * lat
    tg_ref[...] = bias[0:own, 0:width].astype(LOW)
    if staged:
        for p in range(pairs):
            finish(p)


def body(n, tokens, input_weight, output_weight, upstream):
    lat, cols, width = tokens.shape
    own = lat * cols
    parts = segments(cols)
    rim = lat * sum(part[1] for part in parts)
    total = own + rim
    rows = width // n
    staged = rows % 16 == 0 and n % 4 == 0 and n > 8
    x = tokens.transpose(1, 0, 2).reshape(own, width)
    u = upstream.transpose(1, 0, 2).reshape(own, width)
    pairs = width // 128
    vmem = pl.BlockSpec(memory_space=pltpu.VMEM)
    out_shape = [jax.ShapeDtypeStruct((own, width), LOW)]
    scratch = [
        pltpu.VMEM((total, width), LOW),
        pltpu.VMEM((width, total), LOW),
        pltpu.VMEM((width, own), LOW),
        pltpu.VMEM((total, 2 * width), LOW),
        pltpu.VMEM((own, width), LOW),
        pltpu.VMEM((own, width), LOW),
        pltpu.VMEM((own, width), LOW),
        pltpu.VMEM((total, 2 * width), LOW),
        pltpu.VMEM((2 * own, total), F32),
        pltpu.VMEM((rim, width), LOW),
        pltpu.VMEM((rim, width), LOW),
    ] + [pltpu.SemaphoreType.DMA((len(parts),))] * 4
    if staged:
        deep = n // 4
        out_shape += [
            jax.ShapeDtypeStruct((rows, 3 * width), F32),
            jax.ShapeDtypeStruct((rows, width), F32),
        ]
        scratch += [
            pltpu.VMEM((pairs, 2, 2 * deep, rows, 512), LOW),
            pltpu.VMEM((pairs, 2 * deep, rows, 512), LOW),
            pltpu.VMEM((pairs, 2, deep, rows, 512), LOW),
            pltpu.VMEM((pairs, deep, rows, 512), LOW),
            pltpu.VMEM((pairs, deep, rows, 512), LOW),
            pltpu.VMEM((pairs, deep - 1, rows, 512), LOW),
        ]
        scratch += [pltpu.SemaphoreType.DMA((pairs,))] * 4
        scratch += [pltpu.SemaphoreType.DMA((pairs, deep - 1))] * 2
    else:
        out_shape += [jax.ShapeDtypeStruct((width, 4 * width), F32)]
    results = pl.pallas_call(
        functools.partial(kernel, n, lat, cols, staged),
        out_shape=out_shape,
        in_specs=[vmem] * 4,
        out_specs=[vmem] * len(out_shape),
        scratch_shapes=scratch,
        compiler_params=pltpu.CompilerParams(
            collective_id=0, has_side_effects=True, vmem_limit_bytes=56 * 1024 * 1024
        ),
    )(x, u, input_weight, output_weight)
    token_grads = results[0].reshape(cols, lat, width).transpose(1, 0, 2)
    if staged:
        return token_grads, results[1], results[2].T
    term = results[1]
    input_grads = lax.psum_scatter(term[:, : 3 * width], "lon", scatter_dimension=0, tiled=True)
    output_grads = lax.psum_scatter(term[:, 3 * width :].T, "lon", scatter_dimension=1, tiled=True)
    return token_grads, input_grads, output_grads


def solution(mesh):
    in_specs = (P("groups", "lon", None), P(), P(), P("groups", "lon", None))
    out_specs = (P("groups", "lon", None), P("lon", "groups"), P("groups", "lon"))
    return jax.shard_map(
        functools.partial(body, mesh.shape["lon"]),
        mesh=mesh,
        in_specs=in_specs,
        out_specs=out_specs,
        check_vma=False,
    )
```

```python
import functools

import jax
import jax.numpy as jnp
from jax import lax
from jax.experimental import pallas as pl
from jax.experimental.pallas import tpu as pltpu
from jax.sharding import PartitionSpec as P

HEADS = 8
RADIUS = 10
F32 = jnp.float32
LOW = jnp.bfloat16


def rim_widths(cols):
    hop_count = (RADIUS + cols - 1) // cols
    return [min(cols, RADIUS - (distance - 1) * cols) for distance in range(1, hop_count + 1)]


def segments(cols):
    parts = []
    for distance, count in enumerate(rim_widths(cols), 1):
        parts.append((-distance, count, -(distance - 1) * cols - count, cols - count))
        parts.append((distance, count, distance * cols, 0))
    return parts


def nn(left, right):
    return lax.dot_general(left, right, (((1,), (0,)), ((), ())), preferred_element_type=F32)


def nt(left, right):
    return lax.dot_general(left, right, (((1,), (1,)), ((), ())), preferred_element_type=F32)


def tn(left, right):
    return lax.dot_general(left, right, (((0,), (0,)), ((), ())), preferred_element_type=F32)


def kernel(
    n, lat, cols, staged, x_ref, u_ref, wi_ref, wo_ref, *refs
):
    if staged:
        tg_ref, ig_ref, og_ref = refs[:3]
        refs = refs[3:]
    else:
        tg_ref, term_ref = refs[:2]
        refs = refs[2:]
    xe, xet, ut, kv, qs, gs, dq, dkv, bias, tgs, tgr = refs[:11]
    hs, hr, bs, br = refs[11:15]
    own = lat * cols
    width = x_ref.shape[1]
    parts = segments(cols)
    me = lax.axis_index("lon")
    pairs = width // 128
    half = 64
    scale = half ** (-0.5)

    def at(offset):
        return lax.rem(me + offset + n, n)

    offsets = [part[0] for part in parts]
    if staged:
        tb, ra, sa, rb, sb, rc, sas, sar, sbs, sbr, scs, scr = refs[15:]
        deep = n // 4
        core = lax.rem(me, 2)
        mid = lax.rem(me // 2, 2)
        top = me // 4
        offsets = offsets + [4 * k for k in range(1, deep)]
    barrier = pltpu.get_barrier_semaphore()
    for offset in offsets:
        pl.semaphore_signal(
            barrier, inc=1, device_id={"lon": at(offset)}, device_id_type=pl.DeviceIdType.MESH
        )
    pl.semaphore_wait(barrier, len(offsets))

    def remote(src, dst, send, recv, target):
        return pltpu.make_async_remote_copy(
            src_ref=src,
            dst_ref=dst,
            send_sem=send,
            recv_sem=recv,
            device_id={"lon": target},
            device_id_type=pl.DeviceIdType.MESH,
        )

    near, far = cols * lat, parts[2][1] * lat
    left1, right1, left2, right2 = own, own + near, own + 2 * near, own + 2 * near + far
    total = right2 + far
    side = lax.rem(me, 2)
    sibling = me + 1 - 2 * side
    across = at(2 - 4 * side)
    across_back = at(4 * side - 2)

    def rows_at(first, count):
        return pl.ds(pl.multiple_of(first, 32), count)

    far2 = left2 + side * far
    given = left1 + (near - far) * (1 - side) + near * side
    halo = [
        remote(x_ref, xe.at[pl.ds(left1, near)], hs.at[0], hr.at[0], at(1)),
        remote(x_ref, xe.at[pl.ds(right1, near)], hs.at[1], hr.at[1], at(-1)),
        remote(
            x_ref.at[rows_at((near - far) * (1 - side), far)],
            xe.at[rows_at(far2, far)],
            hs.at[2],
            hr.at[2],
            across,
        ),
    ]
    for copy in halo:
        copy.start()

    x_own = x_ref[...]
    xe[0:own, :] = x_own
    qs[...] = (nn(x_own, wi_ref[:, 0:width]).astype(LOW).astype(F32) * scale).astype(LOW)
    gs[...] = nt(u_ref[...], wo_ref[...]).astype(LOW)
    ut[...] = u_ref[...].T
    kv[0:own, :] = nn(x_own, wi_ref[:, width:]).astype(LOW)

    rows2 = lax.broadcasted_iota(jnp.int32, (2 * own, total), 0)
    keys2 = lax.broadcasted_iota(jnp.int32, (2 * own, total), 1)
    rows2 = jnp.where(rows2 >= own, rows2 - own, rows2)
    tile = lax.div(keys2, lat)
    place = tile
    count_before = cols
    for hop, count, first, _ in parts:
        place = jnp.where(tile >= count_before, tile + (first - count_before), place)
        count_before += count
    near_col = jnp.abs(lax.div(rows2, lat) - place) <= RADIUS
    near_lat = jnp.abs(lax.rem(rows2, lat) - lax.rem(keys2, lat)) <= RADIUS
    bias[...] = jnp.where(near_col & near_lat, 0.0, -1e30).astype(F32)

    remote(
        x_ref, xe.at[rows_at(left1 + near * side, near)], hs.at[side], hr.at[side], at(1 - 2 * side)
    ).wait_recv()
    hand_on = remote(
        xe.at[rows_at(given, far)], xe.at[rows_at(far2, far)], hs.at[3], hr.at[3], sibling
    )
    hand_on.start()
    remote(
        x_ref,
        xe.at[rows_at(left1 + near * (1 - side), near)],
        hs.at[1 - side],
        hr.at[1 - side],
        at(2 * side - 1),
    ).wait_recv()
    halo[0].wait_send()
    halo[1].wait_send()
    halo[2].wait()
    hand_on.wait()
    kv[own:total, :] = nn(xe[own:total, :], wi_ref[:, width:]).astype(LOW)
    xet[...] = xe[...].T

    if staged:

        def copy_a(p):
            return remote(
                tb.at[p, 1 - core], ra.at[p], sas.at[p], sar.at[p], me + 1 - 2 * core
            )

        def copy_b(p):
            return remote(
                sa.at[p, 1 - mid], rb.at[p], sbs.at[p], sbr.at[p], me + 2 - 4 * mid
            )

        def copies_c(p):
            out = []
            for k in range(1, deep):
                target = lax.rem(top + k, deep)
                out.append(
                    remote(
                        sb.at[p, target],
                        rc.at[p, k - 1],
                        scs.at[p, k - 1],
                        scr.at[p, k - 1],
                        target * 4 + lax.rem(me, 4),
                    )
                )
            return out

        def stage_b(p):
            copy_a(p).wait()
            mine = tb[p, core].astype(F32) + ra[p].astype(F32)
            sa[p] = mine.astype(LOW).reshape(sa.shape[1:])
            copy_b(p).start()

        def stage_c(p):
            copy_b(p).wait()
            sb[p] = (sa[p, mid].astype(F32) + rb[p].astype(F32)).astype(LOW)
            for copy in copies_c(p):
                copy.start()

        def finish(p):
            for copy in copies_c(p):
                copy.wait()
            done = sa[p, mid, top].astype(F32) + rb[p, top].astype(F32)
            for k in range(1, deep):
                done = done + rc[p, k - 1].astype(F32)
            for k in range(3):
                ig_ref[:, width * k + 128 * p : width * k + 128 * p + 128] = done[
                    :, 128 * k : 128 * k + 128
                ]
            og_ref[:, 128 * p : 128 * p + 128] = done[:, 384:512]

    lane = lax.broadcasted_iota(jnp.int32, (own, 128), 1)

    def stacked(block):
        zero = jnp.zeros_like(block)
        return jnp.concatenate(
            [jnp.where(lane < half, block, zero), jnp.where(lane < half, zero, block)], axis=0
        )

    def picked(block):
        return jnp.where(lane < half, block[0:own], block[own : 2 * own])

    def pair(p, carry):
        here = pl.ds(pl.multiple_of(p * 128, 128), 128)
        there = pl.ds(pl.multiple_of(width + p * 128, 128), 128)
        q2 = stacked(qs[:, here])
        g2 = stacked(gs[:, here])
        k2 = kv[:, here]
        v2 = kv[:, there]
        score = nt(q2, k2) + bias[...]
        peak = jnp.max(score, axis=1, keepdims=True)
        grown = jnp.exp(score - peak)
        probs = grown * (1.0 / jnp.sum(grown, axis=1, keepdims=True))
        low = probs.astype(LOW)
        reached = nn(low, v2).astype(LOW)
        delta = jnp.sum(g2.astype(F32) * reached.astype(F32), axis=1, keepdims=True)
        slope = (probs * (nt(g2, v2) - delta)).astype(LOW)
        dq_p = (picked(nn(slope, k2)) * scale).astype(LOW)
        att_p = picked(reached)
        dk_p = tn(q2, slope).T.astype(LOW)
        dv_p = tn(g2, low).T.astype(LOW)
        dq[:, here] = dq_p
        dkv[:, here] = dk_p
        dkv[:, there] = dv_p
        term_q = nn(xet[:, 0:own], dq_p)
        term_k = nn(xet[...], dk_p)
        term_v = nn(xet[...], dv_p)
        term_o = nn(ut[...], att_p)
        terms = (term_q, term_k, term_v, term_o)
        if staged:
            rows = width // n
            for k, term in enumerate(terms):
                block = term.astype(LOW)
                for j in range(n):
                    tb[p, j % 2, ((j // 2) % 2) * deep + j // 4, :, 128 * k : 128 * k + 128] = (
                        block[rows * j : rows * j + rows]
                    )
            copy_a(p).start()

            @pl.when(p >= 1)
            def _():
                stage_b(p - 1)

            @pl.when(p >= 2)
            def _():
                stage_c(p - 2)
        else:
            for k, term in enumerate(terms):
                term_ref[:, pl.ds(pl.multiple_of(width * k + p * 128, 128), 128)] = term
        return carry

    lax.fori_loop(0, pairs, pair, 0)

    handed = left2 + (1 - side) * far
    tgs[2 * near : 2 * near + far, :] = nt(dkv[rows_at(handed, far), :], wi_ref[:, width:]).astype(LOW)
    hand_back = remote(
        tgs.at[pl.ds(2 * near, far)], tgr.at[pl.ds(2 * near, far)], bs.at[3], br.at[3], sibling
    )
    hand_back.start()
    bias[0 : 2 * near, 0:width] = nt(dkv[left1:left2, :], wi_ref[:, width:])
    tgs[2 * near + far : 2 * near + 2 * far, :] = nt(
        dkv[rows_at(far2, far), :], wi_ref[:, width:]
    ).astype(LOW)
    if staged:
        stage_b(pairs - 1)
    cross = remote(
        tgs.at[pl.ds(2 * near + far, far)],
        tgr.at[pl.ds(2 * near + far, far)],
        bs.at[2],
        br.at[2],
        across_back,
    )
    cross.start()
    hand_back.wait()
    bias[rows_at(given - own, far), 0:width] += tgr[2 * near : 2 * near + far, :].astype(F32)
    tgs[0 : 2 * near, :] = bias[0 : 2 * near, 0:width].astype(LOW)
    back = [
        remote(tgs.at[pl.ds(0, near)], tgr.at[pl.ds(0, near)], bs.at[0], br.at[0], at(-1)),
        remote(tgs.at[pl.ds(near, near)], tgr.at[pl.ds(near, near)], bs.at[1], br.at[1], at(1)),
    ]
    for copy in back:
        copy.start()
    if staged:
        stage_c(pairs - 2)
    mine = nt(dkv[0:own, :], wi_ref[:, width:]) + nt(dq[...], wi_ref[:, 0:width])
    bias[0:own, 0:width] = mine
    if staged:
        stage_c(pairs - 1)
    cross.wait()
    bias[rows_at((near - far) * (1 - side), far), 0:width] += tgr[
        2 * near + far : 2 * near + 2 * far, :
    ].astype(F32)
    for copy in back:
        copy.wait()
    bias[0:own, 0:width] += tgr[0:near, :].astype(F32) + tgr[near : 2 * near, :].astype(F32)
    tg_ref[...] = bias[0:own, 0:width].astype(LOW)
    if staged:
        for p in range(pairs):
            finish(p)


def place(tg_ref, ig_ref, og_ref, tg_out, ig_out, og_out):
    tg_out[...] = tg_ref[...]
    ig_out[...] = ig_ref[...]
    og_out[...] = og_ref[...]


def body(n, tokens, input_weight, output_weight, upstream):
    lat, cols, width = tokens.shape
    own = lat * cols
    parts = segments(cols)
    rim = lat * sum(part[1] for part in parts)
    total = own + rim
    rows = width // n
    staged = rows % 16 == 0 and n % 4 == 0 and n > 8
    x = tokens.transpose(1, 0, 2).reshape(own, width)
    u = upstream.transpose(1, 0, 2).reshape(own, width)
    pairs = width // 128
    vmem = pl.BlockSpec(memory_space=pltpu.VMEM)
    out_shape = [jax.ShapeDtypeStruct((own, width), LOW)]
    scratch = [
        pltpu.VMEM((total, width), LOW),
        pltpu.VMEM((width, total), LOW),
        pltpu.VMEM((width, own), LOW),
        pltpu.VMEM((total, 2 * width), LOW),
        pltpu.VMEM((own, width), LOW),
        pltpu.VMEM((own, width), LOW),
        pltpu.VMEM((own, width), LOW),
        pltpu.VMEM((total, 2 * width), LOW),
        pltpu.VMEM((2 * own, total), F32),
        pltpu.VMEM((rim, width), LOW),
        pltpu.VMEM((rim, width), LOW),
    ] + [pltpu.SemaphoreType.DMA((len(parts),))] * 4
    if staged:
        deep = n // 4
        out_shape += [
            jax.ShapeDtypeStruct((rows, 3 * width), F32),
            jax.ShapeDtypeStruct((rows, width), F32),
        ]
        scratch += [
            pltpu.VMEM((pairs, 2, 2 * deep, rows, 512), LOW),
            pltpu.VMEM((pairs, 2 * deep, rows, 512), LOW),
            pltpu.VMEM((pairs, 2, deep, rows, 512), LOW),
            pltpu.VMEM((pairs, deep, rows, 512), LOW),
            pltpu.VMEM((pairs, deep, rows, 512), LOW),
            pltpu.VMEM((pairs, deep - 1, rows, 512), LOW),
        ]
        scratch += [pltpu.SemaphoreType.DMA((pairs,))] * 4
        scratch += [pltpu.SemaphoreType.DMA((pairs, deep - 1))] * 2
    else:
        out_shape += [jax.ShapeDtypeStruct((width, 4 * width), F32)]
    results = pl.pallas_call(
        functools.partial(kernel, n, lat, cols, staged),
        out_shape=out_shape,
        in_specs=[vmem] * 4,
        out_specs=[vmem] * len(out_shape),
        scratch_shapes=scratch,
        compiler_params=pltpu.CompilerParams(
            collective_id=0, has_side_effects=True, vmem_limit_bytes=56 * 1024 * 1024
        ),
    )(x, u, input_weight, output_weight)
    if staged:
        results = pl.pallas_call(
            place,
            out_shape=[
                jax.ShapeDtypeStruct((own, width), LOW),
                jax.ShapeDtypeStruct((rows, 3 * width), F32),
                jax.ShapeDtypeStruct((rows, width), F32),
            ],
            in_specs=[vmem] * 3,
            out_specs=[vmem] * 3,
        )(*results)
    token_grads = results[0].reshape(cols, lat, width).transpose(1, 0, 2)
    if staged:
        return token_grads, results[1], results[2].T
    term = results[1]
    input_grads = lax.psum_scatter(term[:, : 3 * width], "lon", scatter_dimension=0, tiled=True)
    output_grads = lax.psum_scatter(term[:, 3 * width :].T, "lon", scatter_dimension=1, tiled=True)
    return token_grads, input_grads, output_grads


def solution(mesh):
    in_specs = (P("groups", "lon", None), P(), P(), P("groups", "lon", None))
    out_specs = (P("groups", "lon", None), P("lon", "groups"), P("groups", "lon"))
    return jax.shard_map(
        functools.partial(body, mesh.shape["lon"]),
        mesh=mesh,
        in_specs=in_specs,
        out_specs=out_specs,
        check_vma=False,
    )
```
